256 devices in a mesh: pt: 8 (over x, z_hi), pan: 32 (over y, z_lo, core).
Axes of the slice: x: 4, y: 4, z: 8 (z_hi: 2, z_lo: 4; z = z_hi * 4 + z_lo), core: 2. Of those that a mesh axis runs over, the one named last changes fastest.
Arguments:
- potential: bfloat16 [8, 6144, 6144], P('pt', 'pan'), may hold values from -6 to 6
- basis: bfloat16 [6144, 1280], P(None, 'pan'), may hold values from -0.078125 to 0.078125
- weights: float32 [8], replicated, may hold values from 0.05 to 0.3
- coupling: float32 [8, 8], replicated, may hold values from -0.03 to 0.03
Outputs:
- exponent: float32 [1280, 1280], P('pan', 'pt')
The draws below stay inside these ranges and needn't reach their ends.
All inputs are finite; a program needn't handle non-finite values.
Results may differ from the reference program's by a relative error of at most 0.02.
Values may be sent and summed in bfloat16 or wider, within the bound.
No kernel may reach another device: no remote copies, remote signals or barrier semaphores. Data moves between devices by JAX's collectives and lax.ppermute only.
A program may use at most 64 MiB of HBM per device.

```python
import jax
import jax.numpy as jnp

NB = 6144
NC = 1280
Q = 8


def block_levels(own_key, extent, pieces, least, top_value):
    def one(axis_at, blocks):
        draws = jax.random.uniform(jax.random.fold_in(jax.random.fold_in(own_key, 6), axis_at), (blocks,), jnp.float32, least / len(pieces), top_value / len(pieces))
        return jnp.repeat(jnp.exp(draws), extent[axis_at] // blocks).reshape((-1,) + (1,) * (len(extent) - axis_at - 1))

    loudness = one(*pieces[0])
    for cut in pieces[1:]:
        loudness = loudness * one(*cut)
    return loudness


def bell_draw(stream_key, shape, width, bound, split=(), held_as=jnp.bfloat16):
    entries = jax.random.normal(stream_key, shape, jnp.float32) * width
    if len(split) > 0:
        entries = block_levels(stream_key, shape, split, -0.22, 0.18) * entries
    return jnp.clip(entries, min=-bound, max=bound).astype(held_as)


def setup_inputs(seed: int = 0) -> dict:
    streams_of = jax.random.split(jax.random.key(seed), 5)
    potential = bell_draw(streams_of[0], (Q, NB, NB), 1.0, 6.0, ((0, 8), (1, 32)))
    basis = bell_draw(streams_of[1], (NB, NC), NB ** -0.5, 0.078125, ((1, 32),))
    weights = jnp.clip(jax.random.uniform(streams_of[2], (Q,), jnp.float32, 0.05, 0.3), 0.05, 0.3)
    coupling = bell_draw(streams_of[3], (Q, Q), 0.005, 0.03, (), jnp.float32)
    return dict(potential=potential, basis=basis, weights=weights, coupling=coupling)


def reference(potential, basis, weights, coupling):
    antisym = coupling - coupling.T
    layers = []
    for point in range(Q):
        projected = jnp.dot(potential[point], basis, preferred_element_type=jnp.float32).astype(jnp.bfloat16)
        layers.append(jnp.dot(projected.T, basis, preferred_element_type=jnp.float32).astype(jnp.bfloat16))
    stacked = jnp.stack(layers)
    widened = stacked.astype(jnp.float32)
    total = jnp.einsum('q,qij->ij', weights.astype(jnp.float32), widened)
    for point in range(Q):
        mixed = jnp.einsum('r,rij->ij', antisym[point].astype(jnp.float32), widened).astype(jnp.bfloat16)
        total = total + jnp.dot(mixed, stacked[point], preferred_element_type=jnp.float32)
    return total
```

```python
import jax
import jax.numpy as jnp
from jax import lax
from jax.sharding import PartitionSpec as P

BF = jnp.bfloat16
F32 = jnp.float32
AXES = ("pt", "pan")


def place(x, y, z, c):
    return ((x % 4) * 2 + (z % 8) // 4) * 32 + (y % 4) * 8 + (z % 4) * 2 + c


def pairs(move):
    return [
        (place(x, y, z, c), place(*move(x, y, z, c)))
        for x in range(4) for y in range(4) for z in range(8) for c in range(2)
    ]


def along(first, ring):
    def z_move(z, step):
        return z + step if ring else z // 4 * 4 + (z + step) % 4

    def perm(step):
        return pairs(
            lambda x, y, z, c: (x, y, z_move(z, step(z)), c) if (c == 0) == first else (x, y + step(y), z, c)
        )

    return perm


UP = lambda v: 1
DOWN = lambda v: -1
TWO = lambda v: 2 if v % 2 == 0 else -2
CORE = pairs(lambda x, y, z, c: (x, y, z, 1 - c))
CHIPS = [[2 * chip + core for chip in range(16)] for core in range(2)]


def send(value, perm):
    return lax.ppermute(value, AXES, perm)


def gather_line(value, axis):
    up = send(value, axis(UP))
    down = send(value, axis(DOWN))
    two = send(value, axis(TWO))
    return value, down, two, up


def nt(a, b):
    return lax.dot_general(a, b, (((1,), (1,)), ((), ())), preferred_element_type=F32)


def unroll(blocks, start):
    return lax.dynamic_slice_in_dim(jnp.concatenate([blocks, blocks], 0), (4 - start) % 4, 4, 0)


def shards(potential, basis, weights, coupling):
    point = lax.axis_index("pt")
    pan = lax.axis_index("pan")
    core = pan % 2
    chip = pan // 2
    y, z = chip // 4, chip % 4
    second = jnp.where(core == 0, y, z)
    first = jnp.where(core == 0, z, y)
    rows = potential[0]
    panel = basis.T
    width, depth = panel.shape

    with jax.named_scope("basis_line"):
        line = jnp.concatenate(gather_line(panel, along(True, True)), 0)
    with jax.named_scope("rows_pair"):
        other_rows = send(rows, CORE)
        chip_rows = jnp.where(
            core == 0, jnp.concatenate([rows, other_rows], 0), jnp.concatenate([other_rows, rows], 0)
        )
    with jax.named_scope("basis_plane"):
        units = gather_line(line, along(False, True))
    with jax.named_scope("projected"):
        parts = [unroll(nt(u, chip_rows).astype(BF).reshape(4, width, -1), first) for u in units]
        blocks = unroll(jnp.stack(parts), second)
        blocks = jnp.where(core == 0, blocks, blocks.transpose(1, 0, 2, 3)).reshape(16, width, -1)
    with jax.named_scope("projected_exchange"):
        got = lax.all_to_all(blocks, "pan", 0, 0, axis_index_groups=CHIPS, tiled=True)
        own = got.transpose(1, 0, 2).reshape(width, depth)
        both = jnp.concatenate([own, send(own, CORE)], 0)
    with jax.named_scope("channel"):
        channel = jnp.concatenate([nt(both, u).astype(BF) for u in units], 1)
    with jax.named_scope("points"):
        every = lax.all_to_all(jnp.broadcast_to(channel, (8,) + channel.shape), "pt", 0, 0, tiled=True)
        every = every.reshape(8, 2 * width, 16 * width)
        every_other = send(every, CORE)
    with jax.named_scope("select"):
        lane = jnp.arange(2 * width)
        want = 2 * point + lane // width
        dy, dz = (want // 4 - y) % 4, (want % 4 - z) % 4
        spot = (jnp.where(core == 0, dy * 4 + dz, dz * 4 + dy)) * width + lane % width
        pick = (jnp.arange(16 * width)[:, None] == spot[None, :]).astype(BF)
        chosen = jnp.dot(every.reshape(-1, 16 * width), pick, preferred_element_type=F32)
        chosen = chosen.reshape(8, 2 * width, 2 * width)
        antisym = coupling - coupling.T
        mixed = jnp.einsum("qr,qin->irn", antisym, chosen, precision=lax.Precision.HIGHEST)
        mixed = mixed.astype(BF).reshape(2 * width, -1)
        linear = jnp.einsum("q,qin->in", weights, chosen, precision=lax.Precision.HIGHEST)
    with jax.named_scope("mixed_gather"):
        mline = jnp.concatenate(gather_line(mixed, along(True, False)), 0)
        mplane = jnp.stack(gather_line(mline, along(False, False)))
    with jax.named_scope("product"):
        right = mplane.reshape(4, 4, 2, width, 8, 2 * width)
        right_own = right[:, :, 0].transpose(3, 0, 1, 2, 4).reshape(8, 16 * width, 2 * width)
        right_other = right[:, :, 1].transpose(3, 1, 0, 2, 4).reshape(8, 16 * width, 2 * width)
        total, crossed = linear, 0.0
        for r in range(8):
            total = total + jnp.dot(every[r], right_own[r], preferred_element_type=F32)
            crossed = crossed + jnp.dot(every_other[r], right_other[r], preferred_element_type=F32)
        total = total + jnp.concatenate([crossed[width:], crossed[:width]], 0)
    with jax.named_scope("output"):
        mine = total[:width].reshape(width, 2, 1, width)
        theirs = send(total[width:], CORE).reshape(width, 2, 1, width)
        out = jnp.where(
            core == 0, jnp.concatenate([mine, theirs], 2), jnp.concatenate([theirs, mine], 2)
        )
        return out.reshape(width, 4 * width)


def solution(mesh):
    in_specs = (P("pt", "pan", None), P(None, "pan"), P(), P())
    return jax.shard_map(shards, mesh=mesh, in_specs=in_specs, out_specs=P("pan", "pt"), check_vma=False)
```

```python
import jax
import jax.numpy as jnp
from jax import lax
from jax.experimental import pallas as pl
from jax.experimental.pallas import tpu as pltpu
from jax.sharding import PartitionSpec as P

BF = jnp.bfloat16
F32 = jnp.float32
AXES = ("pt", "pan")


def place(x, y, z, c):
    return ((x % 4) * 2 + (z % 8) // 4) * 32 + (y % 4) * 8 + (z % 4) * 2 + c


def pairs(move):
    return [
        (place(x, y, z, c), place(*move(x, y, z, c)))
        for x in range(4) for y in range(4) for z in range(8) for c in range(2)
    ]


def along(first, ring):
    def z_move(z, step):
        return z + step if ring else z // 4 * 4 + (z + step) % 4

    def perm(step):
        return pairs(
            lambda x, y, z, c: (x, y, z_move(z, step(z)), c) if (c == 0) == first else (x, y + step(y), z, c)
        )

    return perm


UP = lambda v: 1
DOWN = lambda v: -1
TWO = lambda v: 2 if v % 2 == 0 else -2
CORE = pairs(lambda x, y, z, c: (x, y, z, 1 - c))
CHIPS = [[2 * chip + core for chip in range(16)] for core in range(2)]


def send(value, perm):
    return lax.ppermute(value, AXES, perm)


def gather_line(value, axis):
    up = send(value, axis(UP))
    down = send(value, axis(DOWN))
    two = send(value, axis(TWO))
    return value, down, two, up


def nt(a, b):
    return lax.dot_general(a, b, (((1,), (1,)), ((), ())), preferred_element_type=F32)


def unroll(blocks, start):
    return lax.dynamic_slice_in_dim(jnp.concatenate([blocks, blocks], 0), (4 - start) % 4, 4, 0)


INTERPRET = False


def product_kernel(own_ref, other_ref, m0, m1, m2, m3, linear_ref, out_ref, right_own, right_other):
    points, side, _ = own_ref.shape
    half = side // 2
    part = m0.shape[0] // 2
    for a, m in enumerate((m0, m1, m2, m3)):
        right_own[a * part : (a + 1) * part] = m[:part]
        right_other[a * part : (a + 1) * part] = m[part:]
    total = linear_ref[...]
    crossed = jnp.zeros((side, side), F32)
    for r in range(points):
        low = side * r // 128 * 128
        high = min(-(-(side * r + side) // 128) * 128, points * side)
        at = side * r - low
        mine = jnp.dot(own_ref[r], right_own[:, low:high], preferred_element_type=F32)
        total = total + mine[:, at : at + side]
        theirs = jnp.dot(other_ref[r], right_other[:, low:high], preferred_element_type=F32)
        crossed = crossed + theirs[:, at : at + side]
    out_ref[:half] = total[:half] + crossed[half:]
    out_ref[half:] = total[half:] + crossed[:half]


def product(own, other, planes, linear):
    points, side, lanes = own.shape
    return pl.pallas_call(
        product_kernel,
        out_shape=jax.ShapeDtypeStruct((side, side), F32),
        in_specs=[pl.BlockSpec(memory_space=pltpu.VMEM)] * 7,
        out_specs=pl.BlockSpec(memory_space=pltpu.VMEM),
        scratch_shapes=[pltpu.VMEM((lanes, points * side), BF)] * 2,
        compiler_params=pltpu.CompilerParams(vmem_limit_bytes=32 * 1024 * 1024),
        interpret=INTERPRET,
    )(own, other, *planes, linear)


def one_hot(spots, count):
    return (jnp.arange(count)[:, None] == spots[None, :]).astype(BF)


def shards(potential, basis, weights, coupling):
    point = lax.axis_index("pt")
    pan = lax.axis_index("pan")
    core = pan % 2
    chip = pan // 2
    y, z = chip // 4, chip % 4
    second = jnp.where(core == 0, y, z)
    first = jnp.where(core == 0, z, y)
    rows = potential[0]
    panel = basis.T
    width, depth = panel.shape

    with jax.named_scope("basis_line"):
        line = jnp.concatenate(gather_line(panel, along(True, True)), 0)
    with jax.named_scope("rows_pair"):
        other_rows = send(rows, CORE)
        chip_rows = jnp.where(
            core == 0, jnp.concatenate([rows, other_rows], 0), jnp.concatenate([other_rows, rows], 0)
        )
        chip_rows = lax.optimization_barrier(chip_rows)
    with jax.named_scope("basis_plane"):
        units = gather_line(line, along(False, True))
    with jax.named_scope("projected"):
        parts = [unroll(nt(u, chip_rows).astype(BF).reshape(4, width, -1), first) for u in units]
        blocks = unroll(jnp.stack(parts), second)
        blocks = jnp.where(core == 0, blocks, blocks.transpose(1, 0, 2, 3)).reshape(16, width, -1)
    with jax.named_scope("projected_exchange"):
        got = lax.all_to_all(blocks, "pan", 0, 0, axis_index_groups=CHIPS, tiled=True)
        own = got.transpose(1, 0, 2).reshape(width, depth)
        both = jnp.concatenate([own, send(own, CORE)], 0)
    with jax.named_scope("channel"):
        channel = jnp.concatenate([nt(both, u).astype(BF) for u in units], 1)
    lanes, side = 16 * width, 2 * width
    with jax.named_scope("columns_exchange"):
        lane = jnp.arange(lanes)
        want = lane // width
        dy, dz = (want // 4 - y) % 4, (want % 4 - z) % 4
        spot = jnp.where(core == 0, dy * 4 + dz, dz * 4 + dy) * width + lane % width
        sorted_columns = jnp.dot(channel, one_hot(spot, lanes), preferred_element_type=F32).astype(BF)
        sorted_columns = sorted_columns.reshape(side, 8, side).transpose(1, 0, 2)
        chosen = lax.all_to_all(sorted_columns, "pt", 0, 0, tiled=True)
        chosen, channel = lax.optimization_barrier((chosen, channel))
        chosen = chosen.astype(F32)
        antisym = coupling - coupling.T
        mixed = jnp.einsum("qr,qin->irn", antisym, chosen, precision=lax.Precision.HIGHEST)
        mixed = mixed.astype(BF).reshape(side, -1)
        linear = jnp.einsum("q,qin->in", weights, chosen, precision=lax.Precision.HIGHEST)
    with jax.named_scope("mixed_line"):
        line = gather_line(mixed, along(True, False))
        line = jnp.concatenate([m[:width] for m in line] + [m[width:] for m in line], 0)
    with jax.named_scope("points"):
        every = lax.all_to_all(jnp.broadcast_to(channel, (8,) + channel.shape), "pt", 0, 0, tiled=True)
        other = send(every, CORE)
        spot = jnp.arange(lanes).reshape(4, 4, width).transpose(1, 0, 2).reshape(-1)
        other = jnp.dot(other.reshape(-1, lanes), one_hot(spot, lanes), preferred_element_type=F32)
        other = other.astype(BF).reshape(every.shape)
    with jax.named_scope("mixed_plane"):
        planes = gather_line(line, along(False, False))
    with jax.named_scope("product"):
        total = product(every, other, planes, linear)
    with jax.named_scope("output"):
        mine = total[:width].reshape(width, 2, 1, width)
        theirs = send(total[width:], CORE).reshape(width, 2, 1, width)
        out = jnp.where(
            core == 0, jnp.concatenate([mine, theirs], 2), jnp.concatenate([theirs, mine], 2)
        )
        return out.reshape(width, 4 * width)


def solution(mesh):
    in_specs = (P("pt", "pan", None), P(None, "pan"), P(), P())
    return jax.shard_map(shards, mesh=mesh, in_specs=in_specs, out_specs=P("pan", "pt"), check_vma=False)
```

```python
import jax
import jax.numpy as jnp
from jax import lax
from jax.experimental import pallas as pl
from jax.experimental.pallas import tpu as pltpu
from jax.sharding import PartitionSpec as P

BF = jnp.bfloat16
F32 = jnp.float32
AXES = ("pt", "pan")


def place(x, y, z, c):
    return ((x % 4) * 2 + (z % 8) // 4) * 32 + (y % 4) * 8 + (z % 4) * 2 + c


def pairs(move):
    return [
        (place(x, y, z, c), place(*move(x, y, z, c)))
        for x in range(4) for y in range(4) for z in range(8) for c in range(2)
    ]


def along(first, ring):
    def z_move(z, step):
        return z + step if ring else z // 4 * 4 + (z + step) % 4

    def perm(step):
        return pairs(
            lambda x, y, z, c: (x, y, z_move(z, step(z)), c) if (c == 0) == first else (x, y + step(y), z, c)
        )

    return perm


UP = lambda v: 1
DOWN = lambda v: -1
TWO = lambda v: 2 if v % 2 == 0 else -2
CROSS = lambda step: pairs(lambda x, y, z, c: (x + step(x), y, z, c))
CORE = pairs(lambda x, y, z, c: (x, y, z, 1 - c))
CHIPS = [[2 * chip + core for chip in range(16)] for core in range(2)]


def send(value, perm):
    return lax.ppermute(value, AXES, perm)


def gather_line(value, axis):
    up = send(value, axis(UP))
    down = send(value, axis(DOWN))
    two = send(value, axis(TWO))
    return value, down, two, up


def nt(a, b):
    return lax.dot_general(a, b, (((1,), (1,)), ((), ())), preferred_element_type=F32)


def unroll(blocks, start):
    return lax.dynamic_slice_in_dim(jnp.concatenate([blocks, blocks], 0), (4 - start) % 4, 4, 0)


INTERPRET = False


def product_kernel(left_ref, m0, m1, m2, m3, out_ref, right):
    points, side, lanes = left_ref.shape
    part = m0.shape[0]
    span = m0.shape[1] // points
    for a, m in enumerate((m0, m1, m2, m3)):
        right[a * part : (a + 1) * part] = m[...]
    total = jnp.zeros(out_ref.shape, F32)
    for r in range(points):
        low = span * r // 128 * 128
        high = min(-(-(span * r + span) // 128) * 128, points * span)
        at = span * r - low
        term = jnp.dot(left_ref[r], right[:, low:high], preferred_element_type=F32)
        total = total + term[:, at : at + span]
    out_ref[...] = total


def product(left, planes):
    points, side, lanes = left.shape
    return pl.pallas_call(
        product_kernel,
        out_shape=jax.ShapeDtypeStruct((side, planes[0].shape[1] // points), F32),
        in_specs=[pl.BlockSpec(memory_space=pltpu.VMEM)] * 5,
        out_specs=pl.BlockSpec(memory_space=pltpu.VMEM),
        scratch_shapes=[pltpu.VMEM((lanes, planes[0].shape[1]), BF)],
        compiler_params=pltpu.CompilerParams(vmem_limit_bytes=32 * 1024 * 1024),
        interpret=INTERPRET,
    )(left, *planes)


def one_hot(spots, count):
    return (jnp.arange(count)[:, None] == spots[None, :]).astype(BF)


def shards(potential, basis, weights, coupling):
    point = lax.axis_index("pt")
    pan = lax.axis_index("pan")
    core = pan % 2
    chip = pan // 2
    x, y, z = point // 2, chip // 4, chip % 4
    second = jnp.where(core == 0, y, z)
    first = jnp.where(core == 0, z, y)
    rows = potential[0]
    panel = basis.T
    width, depth = panel.shape

    with jax.named_scope("basis_line"):
        line = jnp.concatenate(gather_line(panel, along(True, True)), 0)
    with jax.named_scope("rows_pair"):
        line, other_rows = lax.optimization_barrier((line, send(rows, CORE)))
        chip_rows = jnp.where(
            core == 0, jnp.concatenate([rows, other_rows], 0), jnp.concatenate([other_rows, rows], 0)
        )
        chip_rows = lax.optimization_barrier(chip_rows)
    with jax.named_scope("basis_plane"):
        plane = along(False, True)
        fetched = lax.dynamic_index_in_dim(line.reshape(4, width, depth), x, 0, keepdims=False)
        fetched, line = lax.optimization_barrier((send(fetched, plane(TWO)), line))
        two = jnp.zeros((4, width, depth), BF)
        for step, perm in ((0, None), (1, CROSS(DOWN)), (3, CROSS(UP)), (2, CROSS(TWO))):
            piece = fetched if perm is None else send(fetched, perm)
            two = lax.dynamic_update_index_in_dim(two, piece, (x + step) % 4, 0)
        units = line, send(line, plane(DOWN)), two.reshape(4 * width, depth), send(line, plane(UP))
    with jax.named_scope("projected"):
        parts = [unroll(nt(u, chip_rows).astype(BF).reshape(4, width, -1), first) for u in units]
        blocks = unroll(jnp.stack(parts), second)
        blocks = jnp.where(core == 0, blocks, blocks.transpose(1, 0, 2, 3)).reshape(16, width, -1)
    with jax.named_scope("projected_exchange"):
        got = lax.all_to_all(blocks, "pan", 0, 0, axis_index_groups=CHIPS, tiled=True)
        own = got.transpose(1, 0, 2).reshape(width, depth)
        both = jnp.concatenate([own, send(own, CORE)], 0)
    with jax.named_scope("channel"):
        channel = jnp.concatenate([nt(both, u).astype(BF) for u in units], 1)
    lanes = 16 * width
    with jax.named_scope("columns_exchange"):
        crossed = send(channel[width:], CORE)
        block = jnp.arange(2 * lanes) // width
        dy, dz = (block // 8 - y) % 4, (block // 2 % 4 - z) % 4
        spot = jnp.where(block % 2 == 0, dy * 4 + dz, dz * 4 + dy) * width + jnp.arange(2 * lanes) % width
        mine = block % 2 == core
        ordered = jnp.dot(channel[:width], one_hot(jnp.where(mine, spot, -1), lanes), preferred_element_type=F32)
        ordered += jnp.dot(crossed, one_hot(jnp.where(mine, -1, spot), lanes), preferred_element_type=F32)
        ordered = ordered.astype(BF).reshape(width, 8, 4 * width).transpose(1, 0, 2)
        chosen = lax.all_to_all(ordered, "pt", 0, 0, tiled=True)
        chosen, channel = lax.optimization_barrier((chosen, channel))
        chosen = chosen.astype(F32)
        antisym = coupling - coupling.T
        mixed = jnp.einsum("qr,qin->irn", antisym, chosen, precision=lax.Precision.HIGHEST)
        mixed = mixed.astype(BF).reshape(width, -1)
        linear = jnp.einsum("q,qin->in", weights, chosen, precision=lax.Precision.HIGHEST)
    with jax.named_scope("mixed_line"):
        line = jnp.concatenate(gather_line(mixed, along(True, False)), 0)
    with jax.named_scope("points"):
        every = lax.all_to_all(jnp.broadcast_to(channel, (8,) + channel.shape), "pt", 0, 0, tiled=True)
    with jax.named_scope("mixed_plane"):
        planes = gather_line(line, along(False, False))
    with jax.named_scope("product"):
        total = product(every, planes)
    with jax.named_scope("output"):
        return linear + total[:width] + send(total[width:], CORE)


def solution(mesh):
    in_specs = (P("pt", "pan", None), P(None, "pan"), P(), P())
    return jax.shard_map(shards, mesh=mesh, in_specs=in_specs, out_specs=P("pan", "pt"), check_vma=False)
```

```python
import jax
import jax.numpy as jnp
from jax import lax
from jax.experimental import pallas as pl
from jax.experimental.pallas import tpu as pltpu
from jax.sharding import PartitionSpec as P

BF = jnp.bfloat16
F32 = jnp.float32
AXES = ("pt", "pan")


def place(x, y, z, c):
    return ((x % 4) * 2 + (z % 8) // 4) * 32 + (y % 4) * 8 + (z % 4) * 2 + c


def pairs(move):
    return [
        (place(x, y, z, c), place(*move(x, y, z, c)))
        for x in range(4) for y in range(4) for z in range(8) for c in range(2)
    ]


def along(first, ring):
    def z_move(z, step):
        return z + step if ring else z // 4 * 4 + (z + step) % 4

    def perm(step):
        return pairs(
            lambda x, y, z, c: (x, y, z_move(z, step(z)), c) if (c == 0) == first else (x, y + step(y), z, c)
        )

    return perm


UP = lambda v: 1
DOWN = lambda v: -1
TWO = lambda v: 2 if v % 2 == 0 else -2
CROSS = lambda step: pairs(lambda x, y, z, c: (x + step(x), y, z, c))
CORE = pairs(lambda x, y, z, c: (x, y, z, 1 - c))
HALF = pairs(lambda x, y, z, c: (x, y, z + 4, c))
ALONG_X = [[2 * x + half for x in range(4)] for half in range(2)]
CHIPS = [[2 * chip + core for chip in range(16)] for core in range(2)]


def send(value, perm):
    return lax.ppermute(value, AXES, perm)


def gather_line(value, axis):
    up = send(value, axis(UP))
    down = send(value, axis(DOWN))
    two = send(value, axis(TWO))
    return value, down, two, up


def nt(a, b):
    return lax.dot_general(a, b, (((1,), (1,)), ((), ())), preferred_element_type=F32)


def unroll(blocks, start):
    return lax.dynamic_slice_in_dim(jnp.concatenate([blocks, blocks], 0), (4 - start) % 4, 4, 0)


INTERPRET = False


def product_kernel(left_ref, m0, m1, m2, m3, out_ref, right):
    points, side, lanes = left_ref.shape
    part = m0.shape[0]
    span = m0.shape[1] // points
    for a, m in enumerate((m0, m1, m2, m3)):
        right[a * part : (a + 1) * part] = m[...]
    total = jnp.zeros(out_ref.shape, F32)
    for r in range(points):
        low = span * r // 128 * 128
        high = min(-(-(span * r + span) // 128) * 128, points * span)
        at = span * r - low
        term = jnp.dot(left_ref[r], right[:, low:high], preferred_element_type=F32)
        total = total + term[:, at : at + span]
    out_ref[...] = total


def product(left, planes):
    points, side, lanes = left.shape
    return pl.pallas_call(
        product_kernel,
        out_shape=jax.ShapeDtypeStruct((side, planes[0].shape[1] // points), F32),
        in_specs=[pl.BlockSpec(memory_space=pltpu.VMEM)] * 5,
        out_specs=pl.BlockSpec(memory_space=pltpu.VMEM),
        scratch_shapes=[pltpu.VMEM((lanes, planes[0].shape[1]), BF)],
        compiler_params=pltpu.CompilerParams(vmem_limit_bytes=32 * 1024 * 1024),
        interpret=INTERPRET,
    )(left, *planes)


def one_hot(spots, count):
    return (jnp.arange(count)[:, None] == spots[None, :]).astype(BF)


def shards(potential, basis, weights, coupling):
    point = lax.axis_index("pt")
    pan = lax.axis_index("pan")
    core = pan % 2
    chip = pan // 2
    x, y, z = point // 2, chip // 4, chip % 4
    second = jnp.where(core == 0, y, z)
    first = jnp.where(core == 0, z, y)
    rows = potential[0]
    panel = basis.T
    width, depth = panel.shape

    with jax.named_scope("basis_line"):
        line = jnp.concatenate(gather_line(panel, along(True, True)), 0)
    with jax.named_scope("rows_pair"):
        line, other_rows = lax.optimization_barrier((line, send(rows, CORE)))
        chip_rows = jnp.where(
            core == 0, jnp.concatenate([rows, other_rows], 0), jnp.concatenate([other_rows, rows], 0)
        )
        chip_rows = lax.optimization_barrier(chip_rows)
    with jax.named_scope("basis_plane"):
        plane = along(False, True)
        fetched = lax.dynamic_index_in_dim(line.reshape(4, width, depth), x, 0, keepdims=False)
        fetched, line = lax.optimization_barrier((send(fetched, plane(TWO)), line))
        two = jnp.zeros((4, width, depth), BF)
        for step, perm in ((0, None), (1, CROSS(DOWN)), (3, CROSS(UP)), (2, CROSS(TWO))):
            piece = fetched if perm is None else send(fetched, perm)
            two = lax.dynamic_update_index_in_dim(two, piece, (x + step) % 4, 0)
        units = line, send(line, plane(DOWN)), two.reshape(4 * width, depth), send(line, plane(UP))
    with jax.named_scope("projected"):
        parts = [unroll(nt(u, chip_rows).astype(BF).reshape(4, width, -1), first) for u in units]
        blocks = unroll(jnp.stack(parts), second)
        blocks = jnp.where(core == 0, blocks, blocks.transpose(1, 0, 2, 3)).reshape(16, width, -1)
    with jax.named_scope("projected_exchange"):
        got = lax.all_to_all(blocks, "pan", 0, 0, axis_index_groups=CHIPS, tiled=True)
        own = got.transpose(1, 0, 2).reshape(width, depth)
        both = jnp.concatenate([own, send(own, CORE)], 0)
    with jax.named_scope("channel"):
        channel = jnp.concatenate([nt(both, u).astype(BF) for u in units], 1)
    lanes = 16 * width
    with jax.named_scope("columns_exchange"):
        crossed, later = lax.optimization_barrier((send(channel[width:], CORE), channel))
        channel_pair = jnp.stack([channel, send(later, HALF)])
        block = jnp.arange(2 * lanes) // width
        dy, dz = (block // 8 - y) % 4, (block // 2 % 4 - z) % 4
        spot = jnp.where(block % 2 == 0, dy * 4 + dz, dz * 4 + dy) * width + jnp.arange(2 * lanes) % width
        mine = block % 2 == core
        ordered = jnp.dot(channel[:width], one_hot(jnp.where(mine, spot, -1), lanes), preferred_element_type=F32)
        ordered += jnp.dot(crossed, one_hot(jnp.where(mine, -1, spot), lanes), preferred_element_type=F32)
        ordered = ordered.astype(BF).reshape(width, 8, 4 * width).transpose(1, 0, 2)
        chosen = lax.all_to_all(ordered, "pt", 0, 0, tiled=True)
        chosen = chosen.astype(F32)
        antisym = coupling - coupling.T
        turned = antisym.reshape(8, 4, 2)[:, :, ::-1].reshape(8, 8)
        turned = jnp.where(point % 2 == 0, antisym, turned)
        mixed = jnp.einsum("qr,qin->irn", turned, chosen, precision=lax.Precision.HIGHEST)
        mixed = mixed.astype(BF).reshape(width, -1)
        linear = jnp.einsum("q,qin->in", weights, chosen, precision=lax.Precision.HIGHEST)
    with jax.named_scope("mixed_line"):
        pieces = list(gather_line(mixed, along(True, False)))
    with jax.named_scope("points"):
        channel_pair, pieces[1] = lax.optimization_barrier((channel_pair, pieces[1]))
        every = jnp.broadcast_to(channel_pair, (4,) + channel_pair.shape)
        every = lax.all_to_all(every, "pt", 0, 0, axis_index_groups=ALONG_X, tiled=True)
        every = every.reshape((8,) + channel.shape)
    with jax.named_scope("mixed_line"):
        line = jnp.concatenate(pieces, 0)
    with jax.named_scope("mixed_plane"):
        planes = gather_line(line, along(False, False))
    with jax.named_scope("product"):
        total = product(every, planes)
    with jax.named_scope("output"):
        return linear + total[:width] + send(total[width:], CORE)


def solution(mesh):
    in_specs = (P("pt", "pan", None), P(None, "pan"), P(), P())
    return jax.shard_map(shards, mesh=mesh, in_specs=in_specs, out_specs=P("pan", "pt"), check_vma=False)
```

```python
import jax
import jax.numpy as jnp
from jax import lax
from jax.experimental import pallas as pl
from jax.experimental.pallas import tpu as pltpu
from jax.sharding import PartitionSpec as P

BF = jnp.bfloat16
F32 = jnp.float32
AXES = ("pt", "pan")


def place(x, y, z, c):
    return ((x % 4) * 2 + (z % 8) // 4) * 32 + (y % 4) * 8 + (z % 4) * 2 + c


def pairs(move):
    return [
        (place(x, y, z, c), place(*move(x, y, z, c)))
        for x in range(4) for y in range(4) for z in range(8) for c in range(2)
    ]


def along(first, ring):
    def z_move(z, step):
        return z + step if ring else z // 4 * 4 + (z + step) % 4

    def perm(step):
        return pairs(
            lambda x, y, z, c: (x, y, z_move(z, step(z)), c) if (c == 0) == first else (x, y + step(y), z, c)
        )

    return perm


UP = lambda v: 1
DOWN = lambda v: -1
TWO = lambda v: 2 if v % 2 == 0 else -2
CROSS = lambda step: pairs(lambda x, y, z, c: (x + step(x), y, z, c))
CORE = pairs(lambda x, y, z, c: (x, y, z, 1 - c))
HALF = pairs(lambda x, y, z, c: (x, y, z + 4, c))
ALONG_X = [[2 * x + half for x in range(4)] for half in range(2)]


def send(value, perm):
    return lax.ppermute(value, AXES, perm)


def gather_line(value, axis):
    up = send(value, axis(UP))
    down = send(value, axis(DOWN))
    two = send(value, axis(TWO))
    return value, down, two, up


def nt(a, b):
    return lax.dot_general(a, b, (((1,), (1,)), ((), ())), preferred_element_type=F32)


INTERPRET = False


def channel_kernel(place_ref, own_ref, other_ref, u0, u1, u2, u3, out_ref, left):
    y, z, core = place_ref[0], place_ref[1], place_ref[2]
    _, _, width, depth = own_ref.shape
    pad = -(-width // 16) * 16
    for first in range(4):
        for second in range(4):
            straight = (y + second) % 4 * 4 + (z + first) % 4
            across = (y + first) % 4 * 4 + (z + second) % 4
            mine = pl.multiple_of(jnp.where(core == 0, straight, across) * depth, depth)
            theirs = pl.multiple_of(jnp.where(core == 0, across, straight) * depth, depth)
            left[:width, pl.ds(mine, depth)] = own_ref[first, second]
            left[pad : pad + width, pl.ds(theirs, depth)] = other_ref[first, second]
    for a, u in enumerate((u0, u1, u2, u3)):
        part = u.shape[0]
        block = nt(left[...], u[...]).astype(BF)
        out_ref[0, :, a * part : (a + 1) * part] = block[:width]
        out_ref[1, :, a * part : (a + 1) * part] = block[pad : pad + width]


def channel_blocks(place_index, own, other, units):
    _, _, width, depth = own.shape
    vmem = pl.BlockSpec(memory_space=pltpu.VMEM)
    return pl.pallas_call(
        channel_kernel,
        out_shape=jax.ShapeDtypeStruct((2, width, 4 * units[0].shape[0]), BF),
        in_specs=[pl.BlockSpec(memory_space=pltpu.SMEM)] + [vmem] * 6,
        out_specs=vmem,
        scratch_shapes=[pltpu.VMEM((2 * (-(-width // 16) * 16), 16 * depth), BF)],
        compiler_params=pltpu.CompilerParams(vmem_limit_bytes=48 * 1024 * 1024),
        interpret=INTERPRET,
    )(place_index, own, other, *units)


def product_kernel(left_ref, m0, m1, m2, m3, out_ref, right):
    points, side, lanes = left_ref.shape
    part = m0.shape[0]
    span = m0.shape[1] // points
    for a, m in enumerate((m0, m1, m2, m3)):
        right[a * part : (a + 1) * part] = m[...]
    total = jnp.zeros(out_ref.shape, F32)
    for r in range(points):
        low = span * r // 128 * 128
        high = min(-(-(span * r + span) // 128) * 128, points * span)
        at = span * r - low
        term = jnp.dot(left_ref[r], right[:, low:high], preferred_element_type=F32)
        total = total + term[:, at : at + span]
    out_ref[...] = total


def product(left, planes):
    points, side, lanes = left.shape
    return pl.pallas_call(
        product_kernel,
        out_shape=jax.ShapeDtypeStruct((side, planes[0].shape[1] // points), F32),
        in_specs=[pl.BlockSpec(memory_space=pltpu.VMEM)] * 5,
        out_specs=pl.BlockSpec(memory_space=pltpu.VMEM),
        scratch_shapes=[pltpu.VMEM((lanes, planes[0].shape[1]), BF)],
        compiler_params=pltpu.CompilerParams(vmem_limit_bytes=32 * 1024 * 1024),
        interpret=INTERPRET,
    )(left, *planes)


def one_hot(spots, count):
    return (jnp.arange(count)[:, None] == spots[None, :]).astype(BF)


def shards(potential, basis, weights, coupling):
    point = lax.axis_index("pt")
    pan = lax.axis_index("pan")
    core = pan % 2
    chip = pan // 2
    x, y, z = point // 2, chip // 4, chip % 4
    rows = potential[0]
    panel = basis.T
    width, depth = panel.shape

    with jax.named_scope("basis_line"):
        line = jnp.concatenate(gather_line(panel, along(True, True)), 0)
    with jax.named_scope("rows_pair"):
        line, other_rows = lax.optimization_barrier((line, send(rows, CORE)))
        chip_rows = jnp.where(
            core == 0, jnp.concatenate([rows, other_rows], 0), jnp.concatenate([other_rows, rows], 0)
        )
        chip_rows = lax.optimization_barrier(chip_rows)
    with jax.named_scope("basis_plane"):
        plane = along(False, True)
        fetched = lax.dynamic_index_in_dim(line.reshape(4, width, depth), x, 0, keepdims=False)
        fetched, line = lax.optimization_barrier((send(fetched, plane(TWO)), line))
        two = jnp.zeros((4, width, depth), BF)
        for step, perm in ((0, None), (1, CROSS(DOWN)), (3, CROSS(UP)), (2, CROSS(TWO))):
            piece = fetched if perm is None else send(fetched, perm)
            two = lax.dynamic_update_index_in_dim(two, piece, (x + step) % 4, 0)
        units = line, send(line, plane(DOWN)), two.reshape(4 * width, depth), send(line, plane(UP))
    with jax.named_scope("projected"):
        back, aside = along(False, False), along(True, False)
        parts = [nt(u, chip_rows).astype(BF).reshape(4, width, -1) for u in units]
    with jax.named_scope("projected_back"):
        parts = parts[0], send(parts[3], back(DOWN)), send(parts[2], back(TWO)), send(parts[1], back(UP))
    with jax.named_scope("projected_aside"):
        parts = [jnp.stack([part[b] for part in parts]) for b in range(4)]
        own = jnp.stack(
            [parts[0], send(parts[3], aside(DOWN)), send(parts[2], aside(TWO)), send(parts[1], aside(UP))]
        )
        other = send(own, CORE)
    with jax.named_scope("channel"):
        channel = channel_blocks(jnp.stack([y, z, core]), own, other, units)
    lanes = 16 * width
    with jax.named_scope("columns_exchange"):
        channel_pair = jnp.stack([channel, send(channel, HALF)])
        crossed = send(channel[1], CORE)
        block = jnp.arange(2 * lanes) // width
        dy, dz = (block // 8 - y) % 4, (block // 2 % 4 - z) % 4
        spot = jnp.where(block % 2 == 0, dy * 4 + dz, dz * 4 + dy) * width + jnp.arange(2 * lanes) % width
        mine = block % 2 == core
        ordered = jnp.dot(channel[0], one_hot(jnp.where(mine, spot, -1), lanes), preferred_element_type=F32)
        ordered += jnp.dot(crossed, one_hot(jnp.where(mine, -1, spot), lanes), preferred_element_type=F32)
        ordered = ordered.astype(BF).reshape(width, 8, 4 * width).transpose(1, 0, 2)
        chosen = lax.all_to_all(ordered, "pt", 0, 0, tiled=True)
        chosen = chosen.astype(F32)
        antisym = coupling - coupling.T
        turned = antisym.reshape(8, 4, 2)[:, :, ::-1].reshape(8, 8)
        turned = jnp.where(point % 2 == 0, antisym, turned)
        mixed = jnp.einsum("qr,qin->irn", turned, chosen, precision=lax.Precision.HIGHEST)
        mixed = mixed.astype(BF).reshape(width, -1)
        linear = jnp.einsum("q,qin->in", weights, chosen, precision=lax.Precision.HIGHEST)
    with jax.named_scope("mixed_line"):
        pieces = list(gather_line(mixed, along(True, False)))
    with jax.named_scope("points"):
        channel_pair, pieces[1] = lax.optimization_barrier((channel_pair, pieces[1]))
        every = jnp.broadcast_to(channel_pair, (4,) + channel_pair.shape)
        every = lax.all_to_all(every, "pt", 0, 0, axis_index_groups=ALONG_X, tiled=True)
        every = every.reshape(8, 2 * width, -1)
    with jax.named_scope("mixed_line"):
        line = jnp.concatenate(pieces, 0)
    with jax.named_scope("mixed_plane"):
        planes = gather_line(line, along(False, False))
    with jax.named_scope("product"):
        total = product(every, planes)
    with jax.named_scope("output"):
        return linear + total[:width] + send(total[width:], CORE)


def solution(mesh):
    in_specs = (P("pt", "pan", None), P(None, "pan"), P(), P())
    return jax.shard_map(shards, mesh=mesh, in_specs=in_specs, out_specs=P("pan", "pt"), check_vma=False)
```

```python
import jax
import jax.numpy as jnp
from jax import lax
from jax.experimental import pallas as pl
from jax.experimental.pallas import tpu as pltpu
from jax.sharding import PartitionSpec as P

BF = jnp.bfloat16
F32 = jnp.float32
AXES = ("pt", "pan")


def place(x, y, z, c):
    return ((x % 4) * 2 + (z % 8) // 4) * 32 + (y % 4) * 8 + (z % 4) * 2 + c


def pairs(move):
    return [
        (place(x, y, z, c), place(*move(x, y, z, c)))
        for x in range(4) for y in range(4) for z in range(8) for c in range(2)
    ]


def along(first, ring):
    def z_move(z, step):
        return z + step if ring else z // 4 * 4 + (z + step) % 4

    def perm(step):
        return pairs(
            lambda x, y, z, c: (x, y, z_move(z, step(z)), c) if (c == 0) == first else (x, y + step(y), z, c)
        )

    return perm


UP = lambda v: 1
DOWN = lambda v: -1
TWO = lambda v: 2 if v % 2 == 0 else -2
CROSS = lambda step: pairs(lambda x, y, z, c: (x + step(x), y, z, c))
CORE = pairs(lambda x, y, z, c: (x, y, z, 1 - c))
HALF = pairs(lambda x, y, z, c: (x, y, z + 4, c))


def send(value, perm):
    return lax.ppermute(value, AXES, perm)


def gather_line(value, axis):
    up = send(value, axis(UP))
    down = send(value, axis(DOWN))
    two = send(value, axis(TWO))
    return value, down, two, up


def nt(a, b):
    return lax.dot_general(a, b, (((1,), (1,)), ((), ())), preferred_element_type=F32)


INTERPRET = False


def channel_kernel(
    place_ref, own_ref, other_ref, u0, u1, u2, u3, out_ref, mine_ref, theirs_ref, left, by_chip, held, sems
):
    y, z, core = place_ref[0], place_ref[1], place_ref[2]
    _, _, width, depth = own_ref.shape
    pad = -(-width // 16) * 16
    copies = [pltpu.make_async_copy(u, held.at[a], sems.at[a]) for a, u in enumerate((u0, u1, u2, u3))]
    for copy in copies:
        copy.start()
    for first in range(4):
        for second in range(4):
            straight = (y + second) % 4 * 4 + (z + first) % 4
            across = (y + first) % 4 * 4 + (z + second) % 4
            mine = pl.multiple_of(jnp.where(core == 0, straight, across) * depth, depth)
            theirs = pl.multiple_of(jnp.where(core == 0, across, straight) * depth, depth)
            left[:width, pl.ds(mine, depth)] = own_ref[first, second]
            left[pad : pad + width, pl.ds(theirs, depth)] = other_ref[first, second]
    columns = []
    for a, copy in enumerate(copies):
        copy.wait()
        column = nt(held[a], left[...])
        columns.append(column)
        for b in range(4):
            straight = (y + a) % 4 * 4 + (z + b) % 4
            across = (y + b) % 4 * 4 + (z + a) % 4
            by_chip[jnp.where(core == 0, straight, across)] = column[b * width : (b + 1) * width]
    block = jnp.concatenate(columns, 0).T
    out_ref[...] = jnp.concatenate([block[:width], block[pad : pad + width]], 0).astype(BF)
    for point in range(8):
        block = jnp.concatenate([by_chip[2 * point], by_chip[2 * point + 1]], 0).T.astype(BF)
        mine_ref[point] = block[:width]
        theirs_ref[point] = block[pad : pad + width]


def channel_blocks(place_index, own, other, units):
    _, _, width, depth = own.shape
    pad = -(-width // 16) * 16
    vmem = pl.BlockSpec(memory_space=pltpu.VMEM)
    part = jax.ShapeDtypeStruct((8, width, 2 * width), BF)
    return pl.pallas_call(
        channel_kernel,
        out_shape=[jax.ShapeDtypeStruct((2 * width, 16 * width), BF), part, part],
        in_specs=[pl.BlockSpec(memory_space=pltpu.SMEM)] + [vmem] * 2 + [pl.BlockSpec(memory_space=pl.ANY)] * 4,
        out_specs=[vmem] * 3,
        scratch_shapes=[
            pltpu.VMEM((2 * pad, 16 * depth), BF),
            pltpu.VMEM((16, width, 2 * pad), F32),
            pltpu.VMEM((4,) + units[0].shape, BF),
            pltpu.SemaphoreType.DMA((4,)),
        ],
        compiler_params=pltpu.CompilerParams(vmem_limit_bytes=24 * 1024 * 1024),
        interpret=INTERPRET,
    )(place_index, own, other, *units)


def product_kernel(place_ref, l0, l1, l2, l3, m0, m1, m2, m3, linear_ref, mine_ref, theirs_ref, right):
    width, span = linear_ref.shape
    part, lanes = m0.shape
    for a, m in enumerate((m0, m1, m2, m3)):
        right[a * part : (a + 1) * part] = m[...]
    total = jnp.zeros((2 * width, span), F32)
    for r in range(8):
        low = span * r // 128 * 128
        high = min(-(-(span * r + span) // 128) * 128, lanes)
        at = span * r - low
        left = (l0, l1, l2, l3)[r // 2]
        term = jnp.dot(left[r % 2], right[:, low:high], preferred_element_type=F32)
        total = total + term[:, at : at + span]

    def in_order(value):
        piece = [value[:, k * span // 4 : (k + 1) * span // 4] for k in range(4)]
        even = jnp.concatenate([piece[0], piece[2], piece[1], piece[3]], 1)
        odd = jnp.concatenate([piece[2], piece[0], piece[3], piece[1]], 1)
        return jnp.where(place_ref[2] == 0, even, odd)

    mine_ref[...] = in_order(total[:width] + linear_ref[...])
    theirs_ref[...] = in_order(total[width:])


def product(place_index, left, planes, linear):
    vmem = pl.BlockSpec(memory_space=pltpu.VMEM)
    return pl.pallas_call(
        product_kernel,
        out_shape=[jax.ShapeDtypeStruct(linear.shape, F32)] * 2,
        in_specs=[pl.BlockSpec(memory_space=pltpu.SMEM)] + [vmem] * 9,
        out_specs=[vmem] * 2,
        scratch_shapes=[pltpu.VMEM((4 * planes[0].shape[0], planes[0].shape[1]), BF)],
        compiler_params=pltpu.CompilerParams(vmem_limit_bytes=12 * 1024 * 1024),
        interpret=INTERPRET,
    )(place_index, *left, *planes, linear)


def shards(potential, basis, weights, coupling):
    point = lax.axis_index("pt")
    pan = lax.axis_index("pan")
    core = pan % 2
    chip = pan // 2
    x, y, z = point // 2, chip // 4, chip % 4
    rows = potential[0]
    panel = basis.T
    width, depth = panel.shape

    with jax.named_scope("basis_line"):
        line = jnp.concatenate(gather_line(panel, along(True, True)), 0)
    with jax.named_scope("rows_pair"):
        line, other_rows = lax.optimization_barrier((line, send(rows, CORE)))
        chip_rows = jnp.where(
            core == 0, jnp.concatenate([rows, other_rows], 0), jnp.concatenate([other_rows, rows], 0)
        )
        chip_rows = lax.optimization_barrier(chip_rows)
    with jax.named_scope("basis_plane"):
        plane = along(False, True)
        fetched = lax.dynamic_index_in_dim(line.reshape(4, width, depth), x, 0, keepdims=False)
        fetched, line = lax.optimization_barrier((send(fetched, plane(TWO)), line))
        two = jnp.zeros((4, width, depth), BF)
        for step, perm in ((0, None), (1, CROSS(DOWN)), (3, CROSS(UP)), (2, CROSS(TWO))):
            piece = fetched if perm is None else send(fetched, perm)
            two = lax.dynamic_update_index_in_dim(two, piece, (x + step) % 4, 0)
        units = line, send(line, plane(DOWN)), two.reshape(4 * width, depth), send(line, plane(UP))
    with jax.named_scope("projected"):
        back, aside = along(False, False), along(True, False)
        project = lambda unit: nt(unit, chip_rows).astype(BF).reshape(4, width, -1)
        parts = [project(units[0]), project(units[1]), None, project(units[3])]
        two, parts[1], parts[3] = lax.optimization_barrier((units[2], parts[1], parts[3]))
        parts[2] = project(two)
    with jax.named_scope("projected_back"):
        parts = parts[0], send(parts[3], back(DOWN)), send(parts[2], back(TWO)), send(parts[1], back(UP))
    with jax.named_scope("projected_aside"):
        parts = [jnp.stack([part[b] for part in parts]) for b in range(4)]
        own = jnp.stack(
            [parts[0], send(parts[3], aside(DOWN)), send(parts[2], aside(TWO)), send(parts[1], aside(UP))]
        )
        other = send(own, CORE)
    with jax.named_scope("channel"):
        place_index = jnp.stack([y, z, core])
        channel, mine, theirs = channel_blocks(place_index, own, other, units)
    with jax.named_scope("columns_exchange"):
        mine = jnp.stack([mine, send(theirs, CORE)], 1)
        left = [jnp.stack([channel, send(channel, HALF)])]
        chosen = lax.all_to_all(mine, "pt", 0, 0, tiled=True).astype(F32)
        antisym = coupling - coupling.T
        offset = jnp.arange(8)
        order = (x + offset // 2) % 4 * 2 + (offset + point) % 2
        turned = jnp.take(antisym, order, axis=1)
        mixed = jnp.einsum("qr,qein->iren", turned, chosen, precision=lax.Precision.HIGHEST)
        mixed = mixed.astype(BF).reshape(width, -1)
        linear = jnp.einsum("q,qein->ien", weights, chosen, precision=lax.Precision.HIGHEST)
        linear = linear.reshape(width, -1)
    with jax.named_scope("points"):
        left = gather_line(left[0], CROSS)
    with jax.named_scope("mixed_line"):
        line = jnp.concatenate(gather_line(mixed, along(True, False)), 0)
    with jax.named_scope("mixed_plane"):
        planes = gather_line(line, along(False, False))
    with jax.named_scope("product"):
        total, rest = product(place_index, left, planes, linear)
    with jax.named_scope("output"):
        return total + send(rest, CORE)


def solution(mesh):
    in_specs = (P("pt", "pan", None), P(None, "pan"), P(), P())
    return jax.shard_map(shards, mesh=mesh, in_specs=in_specs, out_specs=P("pan", "pt"), check_vma=False)
```

```python
import jax
import jax.numpy as jnp
from jax import lax
from jax.experimental import pallas as pl
from jax.experimental.pallas import tpu as pltpu
from jax.sharding import PartitionSpec as P

BF = jnp.bfloat16
F32 = jnp.float32
AXES = ("pt", "pan")


def place(x, y, z, c):
    return ((x % 4) * 2 + (z % 8) // 4) * 32 + (y % 4) * 8 + (z % 4) * 2 + c


def pairs(move):
    return [
        (place(x, y, z, c), place(*move(x, y, z, c)))
        for x in range(4) for y in range(4) for z in range(8) for c in range(2)
    ]


def along(first, ring):
    def z_move(z, step):
        return z + step if ring else z // 4 * 4 + (z + step) % 4

    def perm(step):
        return pairs(
            lambda x, y, z, c: (x, y, z_move(z, step(z)), c) if (c == 0) == first else (x, y + step(y), z, c)
        )

    return perm


UP = lambda v: 1
DOWN = lambda v: -1
TWO = lambda v: 2 if v % 2 == 0 else -2
CROSS = lambda step: pairs(lambda x, y, z, c: (x + step(x), y, z, c))
CORE = pairs(lambda x, y, z, c: (x, y, z, 1 - c))
HALF = pairs(lambda x, y, z, c: (x, y, z + 4, c))
CHIPS = [[2 * chip + core for chip in range(16)] for core in range(2)]


def send(value, perm):
    return lax.ppermute(value, AXES, perm)


def gather_line(value, axis):
    up = send(value, axis(UP))
    down = send(value, axis(DOWN))
    two = send(value, axis(TWO))
    return value, down, two, up


def nt(a, b):
    return lax.dot_general(a, b, (((1,), (1,)), ((), ())), preferred_element_type=F32)


def unroll(blocks, start):
    return lax.dynamic_slice_in_dim(jnp.concatenate([blocks, blocks], 0), (4 - start) % 4, 4, 0)


def by_offset(values, width, axis):
    firsts, rest, down, two, up = values
    own, lower, upper = jnp.split(firsts, (width, 2 * width), axis)
    return [jnp.concatenate(pair, axis) for pair in ((own, rest), (lower, down), (two,), (upper, up))]


INTERPRET = False


def product_kernel(l0, l1, l2, l3, m0, m1, m2, m3, out_ref, right):
    points = 8
    part = m0.shape[0]
    span = m0.shape[1] // points
    for a, m in enumerate((m0, m1, m2, m3)):
        right[a * part : (a + 1) * part] = m[...]
    total = jnp.zeros(out_ref.shape, F32)
    for r in range(points):
        low = span * r // 128 * 128
        high = min(-(-(span * r + span) // 128) * 128, points * span)
        at = span * r - low
        left = (l0, l1, l2, l3)[r // 2]
        term = jnp.dot(left[r % 2], right[:, low:high], preferred_element_type=F32)
        total = total + term[:, at : at + span]
    out_ref[...] = total


def product(left, planes):
    _, side, lanes = left[0].shape
    span = planes[0].shape[1]
    return pl.pallas_call(
        product_kernel,
        out_shape=jax.ShapeDtypeStruct((side, span // 8), F32),
        in_specs=[pl.BlockSpec(memory_space=pltpu.VMEM)] * 8,
        out_specs=pl.BlockSpec(memory_space=pltpu.VMEM),
        scratch_shapes=[pltpu.VMEM((lanes, span), BF)],
        compiler_params=pltpu.CompilerParams(vmem_limit_bytes=12 * 1024 * 1024),
        interpret=INTERPRET,
    )(*left, *planes)


def one_hot(spots, count):
    return (jnp.arange(count)[:, None] == spots[None, :]).astype(BF)


def shards(potential, basis, weights, coupling):
    point = lax.axis_index("pt")
    pan = lax.axis_index("pan")
    core = pan % 2
    chip = pan // 2
    x, y, z = point // 2, chip // 4, chip % 4
    second = jnp.where(core == 0, y, z)
    first = jnp.where(core == 0, z, y)
    rows = potential[0]
    panel = basis.T
    width, depth = panel.shape

    antisym = coupling - coupling.T
    offset = jnp.arange(8)
    order = (x + offset // 2) % 4 * 2 + (offset + point) % 2
    turned = jnp.take(antisym, order, axis=1)
    plane = along(False, True)
    with jax.named_scope("basis_line"):
        pieces = gather_line(panel, along(True, True))
        down, up = send(panel, plane(DOWN)), send(panel, plane(UP))
        *pieces, down, up, turned, own_rows = lax.optimization_barrier((*pieces, down, up, turned, rows))
        rest = jnp.concatenate(pieces[1:], 0)
        other_rows = send(own_rows, CORE)
        fetched = lax.select_n(x, *pieces)
    with jax.named_scope("basis_plane"):
        fetched, rest, other_rows = lax.optimization_barrier((send(fetched, plane(TWO)), rest, other_rows))
        firsts = jnp.concatenate([panel, down, up], 0)
        two = jnp.zeros((4, width, depth), BF)
        for step, perm in ((0, None), (1, CROSS(DOWN)), (3, CROSS(UP)), (2, CROSS(TWO))):
            piece = fetched if perm is None else send(fetched, perm)
            two = lax.dynamic_update_index_in_dim(two, piece, (x + step) % 4, 0)
        two = two.reshape(4 * width, depth)
        units = firsts, rest, send(rest, plane(DOWN)), two, send(rest, plane(UP))
    with jax.named_scope("rows_pair"):
        chip_rows = jnp.where(
            core == 0, jnp.concatenate([rows, other_rows], 0), jnp.concatenate([other_rows, rows], 0)
        )
        chip_rows = lax.optimization_barrier(chip_rows)
    with jax.named_scope("projected"):
        parts = by_offset([nt(unit, chip_rows).astype(BF) for unit in units], width, 0)
        parts = [unroll(part.reshape(4, width, -1), first) for part in parts]
        blocks = unroll(jnp.stack(parts), second)
        blocks = jnp.where(core == 0, blocks, blocks.transpose(1, 0, 2, 3)).reshape(16, width, -1)
    with jax.named_scope("projected_exchange"):
        got = lax.all_to_all(blocks, "pan", 0, 0, axis_index_groups=CHIPS, tiled=True)
        own = got.transpose(1, 0, 2).reshape(width, depth)
        both = jnp.concatenate([own, send(own, CORE)], 0)
    with jax.named_scope("channel"):
        channel = jnp.concatenate(by_offset([nt(both, unit).astype(BF) for unit in units], width, 1), 1)
    lanes = 16 * width
    with jax.named_scope("columns_exchange"):
        left = [jnp.stack([channel, send(channel, HALF)])]
        crossed = send(channel[width:], CORE)
        block = jnp.arange(2 * lanes) // width
        dy, dz = (block // 8 - y) % 4, (block // 2 % 4 - z) % 4
        spot = jnp.where(block % 2 == 0, dy * 4 + dz, dz * 4 + dy) * width + jnp.arange(2 * lanes) % width
        mine = block % 2 == core
        ordered = jnp.dot(channel[:width], one_hot(jnp.where(mine, spot, -1), lanes), preferred_element_type=F32)
        ordered += jnp.dot(crossed, one_hot(jnp.where(mine, -1, spot), lanes), preferred_element_type=F32)
        ordered = ordered.astype(BF).reshape(width, 8, 4 * width).transpose(1, 0, 2)
        chosen = lax.all_to_all(ordered, "pt", 0, 0, tiled=True)
        chosen = chosen.astype(F32)
        mixed = jnp.einsum("qr,qin->irn", turned, chosen, precision=lax.Precision.HIGHEST)
        mixed = mixed.astype(BF).reshape(width, -1)
        linear = jnp.einsum("q,qin->in", weights, chosen, precision=lax.Precision.HIGHEST)
    with jax.named_scope("points"):
        left = gather_line(left[0], CROSS)
    with jax.named_scope("mixed_line"):
        line = jnp.concatenate(gather_line(mixed, along(True, False)), 0)
    with jax.named_scope("mixed_plane"):
        planes = gather_line(line, along(False, False))
    with jax.named_scope("product"):
        total = product(left, planes)
    with jax.named_scope("output"):
        return linear + total[:width] + send(total[width:], CORE)


def solution(mesh):
    in_specs = (P("pt", "pan", None), P(None, "pan"), P(), P())
    return jax.shard_map(shards, mesh=mesh, in_specs=in_specs, out_specs=P("pan", "pt"), check_vma=False)
```

```python
import jax
import jax.numpy as jnp
from jax import lax
from jax.experimental import pallas as pl
from jax.experimental.pallas import tpu as pltpu
from jax.sharding import PartitionSpec as P

BF = jnp.bfloat16
F32 = jnp.float32
AXES = ("pt", "pan")


def place(x, y, z, c):
    return ((x % 4) * 2 + (z % 8) // 4) * 32 + (y % 4) * 8 + (z % 4) * 2 + c


def pairs(move):
    return [
        (place(x, y, z, c), place(*move(x, y, z, c)))
        for x in range(4) for y in range(4) for z in range(8) for c in range(2)
    ]


def along(first, ring):
    def z_move(z, step):
        return z + step if ring else z // 4 * 4 + (z + step) % 4

    def perm(step):
        return pairs(
            lambda x, y, z, c: (x, y, z_move(z, step(z)), c) if (c == 0) == first else (x, y + step(y), z, c)
        )

    return perm


UP = lambda v: 1
DOWN = lambda v: -1
TWO = lambda v: 2 if v % 2 == 0 else -2
CROSS = lambda step: pairs(lambda x, y, z, c: (x + step(x), y, z, c))
CORE = pairs(lambda x, y, z, c: (x, y, z, 1 - c))
HALF = pairs(lambda x, y, z, c: (x, y, z + 4, c))
CHIPS = [[2 * chip + core for chip in range(16)] for core in range(2)]


def send(value, perm):
    return lax.ppermute(value, AXES, perm)


def gather_line(value, axis):
    up = send(value, axis(UP))
    down = send(value, axis(DOWN))
    two = send(value, axis(TWO))
    return value, down, two, up


def nt(a, b):
    return lax.dot_general(a, b, (((1,), (1,)), ((), ())), preferred_element_type=F32)


def unroll(blocks, start):
    return lax.dynamic_slice_in_dim(jnp.concatenate([blocks, blocks], 0), (4 - start) % 4, 4, 0)


INTERPRET = False


def product_kernel(l0, l1, l2, l3, m0, m1, m2, m3, out_ref, right):
    points = 8
    part = m0.shape[0]
    span = m0.shape[1] // points
    for a, m in enumerate((m0, m1, m2, m3)):
        right[a * part : (a + 1) * part] = m[...]
    total = jnp.zeros(out_ref.shape, F32)
    for r in range(points):
        low = span * r // 128 * 128
        high = min(-(-(span * r + span) // 128) * 128, points * span)
        at = span * r - low
        left = (l0, l1, l2, l3)[r // 2]
        term = jnp.dot(left[r % 2], right[:, low:high], preferred_element_type=F32)
        total = total + term[:, at : at + span]
    out_ref[...] = total


def product(left, planes):
    _, side, lanes = left[0].shape
    span = planes[0].shape[1]
    return pl.pallas_call(
        product_kernel,
        out_shape=jax.ShapeDtypeStruct((side, span // 8), F32),
        in_specs=[pl.BlockSpec(memory_space=pltpu.VMEM)] * 8,
        out_specs=pl.BlockSpec(memory_space=pltpu.VMEM),
        scratch_shapes=[pltpu.VMEM((lanes, span), BF)],
        compiler_params=pltpu.CompilerParams(vmem_limit_bytes=12 * 1024 * 1024),
        interpret=INTERPRET,
    )(*left, *planes)


def one_hot(spots, count):
    return (jnp.arange(count)[:, None] == spots[None, :]).astype(BF)


def shards(potential, basis, weights, coupling):
    point = lax.axis_index("pt")
    pan = lax.axis_index("pan")
    core = pan % 2
    chip = pan // 2
    x, y, z = point // 2, chip // 4, chip % 4
    second = jnp.where(core == 0, y, z)
    first = jnp.where(core == 0, z, y)
    rows = potential[0]
    panel = basis.T
    width, depth = panel.shape

    antisym = coupling - coupling.T
    offset = jnp.arange(8)
    order = (x + offset // 2) % 4 * 2 + (offset + point) % 2
    turned = jnp.take(antisym, order, axis=1)
    with jax.named_scope("basis_line"):
        line = jnp.concatenate(gather_line(panel, along(True, True)), 0)
    with jax.named_scope("rows_pair"):
        line, other_rows, turned = lax.optimization_barrier((line, send(rows, CORE), turned))
        chip_rows = jnp.where(
            core == 0, jnp.concatenate([rows, other_rows], 0), jnp.concatenate([other_rows, rows], 0)
        )
        chip_rows = lax.optimization_barrier(chip_rows)
    with jax.named_scope("basis_plane"):
        plane = along(False, True)
        fetched = lax.dynamic_index_in_dim(line.reshape(4, width, depth), x, 0, keepdims=False)
        fetched, line = lax.optimization_barrier((send(fetched, plane(TWO)), line))
        two = jnp.zeros((4, width, depth), BF)
        for step, perm in ((0, None), (1, CROSS(DOWN)), (3, CROSS(UP)), (2, CROSS(TWO))):
            piece = fetched if perm is None else send(fetched, perm)
            two = lax.dynamic_update_index_in_dim(two, piece, (x + step) % 4, 0)
        units = line, send(line, plane(DOWN)), two.reshape(4 * width, depth), send(line, plane(UP))
    with jax.named_scope("projected"):
        parts = [unroll(nt(u, chip_rows).astype(BF).reshape(4, width, -1), first) for u in units]
        blocks = unroll(jnp.stack(parts), second)
        blocks = jnp.where(core == 0, blocks, blocks.transpose(1, 0, 2, 3)).reshape(16, width, -1)
    with jax.named_scope("projected_exchange"):
        got = lax.all_to_all(blocks, "pan", 0, 0, axis_index_groups=CHIPS, tiled=True)
        own = got.transpose(1, 0, 2).reshape(width, depth)
        both = jnp.concatenate([own, send(own, CORE)], 0)
    with jax.named_scope("channel"):
        channel = jnp.concatenate([nt(both, u).astype(BF) for u in units], 1)
    lanes = 16 * width
    with jax.named_scope("columns_exchange"):
        crossed = send(channel[width:], CORE)
        block = jnp.arange(2 * lanes) // width
        dy, dz = (block // 8 - y) % 4, (block // 2 % 4 - z) % 4
        spot = jnp.where(block % 2 == 0, dy * 4 + dz, dz * 4 + dy) * width + jnp.arange(2 * lanes) % width
        mine = block % 2 == core
        ordered = jnp.dot(channel[:width], one_hot(jnp.where(mine, spot, -1), lanes), preferred_element_type=F32)
        ordered += jnp.dot(crossed, one_hot(jnp.where(mine, -1, spot), lanes), preferred_element_type=F32)
        ordered = ordered.astype(BF).reshape(width, 8, 4 * width).transpose(1, 0, 2)
        chosen = lax.all_to_all(ordered, "pt", 0, 0, tiled=True)
        chosen, channel = lax.optimization_barrier((chosen, channel))
        chosen = chosen.astype(F32)
        mixed = jnp.einsum("qr,qin->irn", turned, chosen, precision=lax.Precision.HIGHEST)
        mixed = mixed.astype(BF).reshape(width, -1)
        linear = jnp.einsum("q,qin->in", weights, chosen, precision=lax.Precision.HIGHEST)
    with jax.named_scope("mixed_line"):
        line = jnp.concatenate(gather_line(mixed, along(True, False)), 0)
        pair = jnp.stack([channel, send(channel, HALF)])
    with jax.named_scope("mixed_plane"):
        line, pair = lax.optimization_barrier((line, pair))
        planes = gather_line(line, along(False, False))
    with jax.named_scope("points"):
        left = gather_line(pair, CROSS)
    with jax.named_scope("product"):
        total = product(left, planes)
    with jax.named_scope("output"):
        return linear + total[:width] + send(total[width:], CORE)


def solution(mesh):
    in_specs = (P("pt", "pan", None), P(None, "pan"), P(), P())
    return jax.shard_map(shards, mesh=mesh, in_specs=in_specs, out_specs=P("pan", "pt"), check_vma=False)
```

```python
import jax
import jax.numpy as jnp
from jax import lax
from jax.experimental import pallas as pl
from jax.experimental.pallas import tpu as pltpu
from jax.sharding import PartitionSpec as P

BF = jnp.bfloat16
F32 = jnp.float32
AXES = ("pt", "pan")


def place(x, y, z, c):
    return ((x % 4) * 2 + (z % 8) // 4) * 32 + (y % 4) * 8 + (z % 4) * 2 + c


def pairs(move):
    return [
        (place(x, y, z, c), place(*move(x, y, z, c)))
        for x in range(4) for y in range(4) for z in range(8) for c in range(2)
    ]


def along(first, ring):
    def z_move(z, step):
        return z + step if ring else z // 4 * 4 + (z + step) % 4

    def perm(step):
        return pairs(
            lambda x, y, z, c: (x, y, z_move(z, step(z)), c) if (c == 0) == first else (x, y + step(y), z, c)
        )

    return perm


UP = lambda v: 1
DOWN = lambda v: -1
TWO = lambda v: 2 if v % 2 == 0 else -2
CROSS = lambda step: pairs(lambda x, y, z, c: (x + step(x), y, z, c))
CORE = pairs(lambda x, y, z, c: (x, y, z, 1 - c))
def far(x, y, z, c):
    back = lambda v: v + (0, -1, TWO(v), 1)[x]
    return (x, y + TWO(y), back(z), c) if c == 0 else (x, back(y), z + TWO(z), c)


FAR = pairs(far)
HALF = pairs(lambda x, y, z, c: (x, y, z + 4, c))
CHIPS = [[2 * chip + core for chip in range(16)] for core in range(2)]


def send(value, perm):
    return lax.ppermute(value, AXES, perm)


def gather_line(value, axis):
    up = send(value, axis(UP))
    down = send(value, axis(DOWN))
    two = send(value, axis(TWO))
    return value, down, two, up


def nt(a, b):
    return lax.dot_general(a, b, (((1,), (1,)), ((), ())), preferred_element_type=F32)


def unroll(blocks, start):
    return lax.dynamic_slice_in_dim(jnp.concatenate([blocks, blocks], 0), (4 - start) % 4, 4, 0)


INTERPRET = False


def product_kernel(l0, l1, l2, l3, m0, m1, m2, m3, out_ref, right):
    points = 8
    part = m0.shape[0]
    span = m0.shape[1] // points
    for a, m in enumerate((m0, m1, m2, m3)):
        right[a * part : (a + 1) * part] = m[...]
    total = jnp.zeros(out_ref.shape, F32)
    for r in range(points):
        low = span * r // 128 * 128
        high = min(-(-(span * r + span) // 128) * 128, points * span)
        at = span * r - low
        left = (l0, l1, l2, l3)[r // 2]
        term = jnp.dot(left[r % 2], right[:, low:high], preferred_element_type=F32)
        total = total + term[:, at : at + span]
    out_ref[...] = total


def product(left, planes):
    _, side, lanes = left[0].shape
    span = planes[0].shape[1]
    return pl.pallas_call(
        product_kernel,
        out_shape=jax.ShapeDtypeStruct((side, span // 8), F32),
        in_specs=[pl.BlockSpec(memory_space=pltpu.VMEM)] * 8,
        out_specs=pl.BlockSpec(memory_space=pltpu.VMEM),
        scratch_shapes=[pltpu.VMEM((lanes, span), BF)],
        compiler_params=pltpu.CompilerParams(vmem_limit_bytes=12 * 1024 * 1024),
        interpret=INTERPRET,
    )(*left, *planes)


def one_hot(spots, count):
    return (jnp.arange(count)[:, None] == spots[None, :]).astype(BF)


def shards(potential, basis, weights, coupling):
    point = lax.axis_index("pt")
    pan = lax.axis_index("pan")
    core = pan % 2
    chip = pan // 2
    x, y, z = point // 2, chip // 4, chip % 4
    second = jnp.where(core == 0, y, z)
    first = jnp.where(core == 0, z, y)
    rows = potential[0]
    panel = basis.T
    width, depth = panel.shape

    antisym = coupling - coupling.T
    offset = jnp.arange(8)
    order = (x + offset // 2) % 4 * 2 + (offset + point) % 2
    turned = jnp.take(antisym, order, axis=1)
    with jax.named_scope("basis_line"):
        line = jnp.concatenate(gather_line(panel, along(True, True)), 0)
    with jax.named_scope("rows_pair"):
        line, fetched, other_rows, turned = lax.optimization_barrier(
            (line, send(panel, FAR), send(rows, CORE), turned)
        )
        chip_rows = jnp.where(
            core == 0, jnp.concatenate([rows, other_rows], 0), jnp.concatenate([other_rows, rows], 0)
        )
        chip_rows = lax.optimization_barrier(chip_rows)
    with jax.named_scope("basis_plane"):
        plane = along(False, True)
        two = jnp.zeros((4, width, depth), BF)
        for step, perm in ((0, None), (1, CROSS(DOWN)), (3, CROSS(UP)), (2, CROSS(TWO))):
            piece = fetched if perm is None else send(fetched, perm)
            two = lax.dynamic_update_index_in_dim(two, piece, (x + step) % 4, 0)
        units = line, send(line, plane(DOWN)), two.reshape(4 * width, depth), send(line, plane(UP))
    with jax.named_scope("projected"):
        parts = [unroll(nt(u, chip_rows).astype(BF).reshape(4, width, -1), first) for u in units]
        blocks = unroll(jnp.stack(parts), second)
        blocks = jnp.where(core == 0, blocks, blocks.transpose(1, 0, 2, 3)).reshape(16, width, -1)
    with jax.named_scope("projected_exchange"):
        got = lax.all_to_all(blocks, "pan", 0, 0, axis_index_groups=CHIPS, tiled=True)
        own = got.transpose(1, 0, 2).reshape(width, depth)
        both = jnp.concatenate([own, send(own, CORE)], 0)
    with jax.named_scope("channel"):
        channel = jnp.concatenate([nt(both, u).astype(BF) for u in units], 1)
    lanes = 16 * width
    with jax.named_scope("columns_exchange"):
        crossed = send(channel[width:], CORE)
        block = jnp.arange(2 * lanes) // width
        dy, dz = (block // 8 - y) % 4, (block // 2 % 4 - z) % 4
        spot = jnp.where(block % 2 == 0, dy * 4 + dz, dz * 4 + dy) * width + jnp.arange(2 * lanes) % width
        mine = block % 2 == core
        ordered = jnp.dot(channel[:width], one_hot(jnp.where(mine, spot, -1), lanes), preferred_element_type=F32)
        ordered += jnp.dot(crossed, one_hot(jnp.where(mine, -1, spot), lanes), preferred_element_type=F32)
        ordered = ordered.astype(BF).reshape(width, 8, 4 * width).transpose(1, 0, 2)
        chosen = lax.all_to_all(ordered, "pt", 0, 0, tiled=True)
        chosen, channel = lax.optimization_barrier((chosen, channel))
        chosen = chosen.astype(F32)
        mixed = jnp.einsum("qr,qin->irn", turned, chosen, precision=lax.Precision.HIGHEST)
        mixed = mixed.astype(BF).reshape(width, -1)
        linear = jnp.einsum("q,qin->in", weights, chosen, precision=lax.Precision.HIGHEST)
    with jax.named_scope("mixed_line"):
        pieces = list(gather_line(mixed, along(True, False)))
        channel, pieces[1] = lax.optimization_barrier((channel, pieces[1]))
        pair = jnp.stack([channel, send(channel, HALF)])
        line = jnp.concatenate(pieces, 0)
    with jax.named_scope("mixed_plane"):
        planes = gather_line(line, along(False, False))
    with jax.named_scope("points"):
        left = gather_line(pair, CROSS)
    with jax.named_scope("product"):
        total = product(left, planes)
    with jax.named_scope("output"):
        return linear + total[:width] + send(total[width:], CORE)


def solution(mesh):
    in_specs = (P("pt", "pan", None), P(None, "pan"), P(), P())
    return jax.shard_map(shards, mesh=mesh, in_specs=in_specs, out_specs=P("pan", "pt"), check_vma=False)
```

```python
import jax
import jax.numpy as jnp
from jax import lax
from jax.experimental import pallas as pl
from jax.experimental.pallas import tpu as pltpu
from jax.sharding import PartitionSpec as P

BF = jnp.bfloat16
F32 = jnp.float32
AXES = ("pt", "pan")


def place(x, y, z, c):
    return ((x % 4) * 2 + (z % 8) // 4) * 32 + (y % 4) * 8 + (z % 4) * 2 + c


def pairs(move):
    return [
        (place(x, y, z, c), place(*move(x, y, z, c)))
        for x in range(4) for y in range(4) for z in range(8) for c in range(2)
    ]


def along(first, ring):
    def z_move(z, step):
        return z + step if ring else z // 4 * 4 + (z + step) % 4

    def perm(step):
        return pairs(
            lambda x, y, z, c: (x, y, z_move(z, step(z)), c) if (c == 0) == first else (x, y + step(y), z, c)
        )

    return perm


UP = lambda v: 1
DOWN = lambda v: -1
TWO = lambda v: 2 if v % 2 == 0 else -2
CROSS = lambda step: pairs(lambda x, y, z, c: (x + step(x), y, z, c))
CORE = pairs(lambda x, y, z, c: (x, y, z, 1 - c))
def far(x, y, z, c):
    back = lambda v: v + (0, -1, TWO(v), 1)[x]
    return (x, y + TWO(y), back(z), c) if c == 0 else (x, back(y), z + TWO(z), c)


FAR = pairs(far)
HALF = pairs(lambda x, y, z, c: (x, y, z + 4, c))
CHIPS = [[2 * chip + core for chip in range(16)] for core in range(2)]


def send(value, perm):
    return lax.ppermute(value, AXES, perm)


def gather_line(value, axis):
    up = send(value, axis(UP))
    down = send(value, axis(DOWN))
    two = send(value, axis(TWO))
    return value, down, two, up


def nt(a, b):
    return lax.dot_general(a, b, (((1,), (1,)), ((), ())), preferred_element_type=F32)


def unroll(blocks, start):
    return lax.dynamic_slice_in_dim(jnp.concatenate([blocks, blocks], 0), (4 - start) % 4, 4, 0)


INTERPRET = False


def product_kernel(l0, l1, l2, l3, m0, m1, m2, m3, out_ref, right):
    points = 8
    part = m0.shape[0]
    span = m0.shape[1] // points
    for a, m in enumerate((m0, m1, m2, m3)):
        right[a * part : (a + 1) * part] = m[...]
    total = jnp.zeros(out_ref.shape, F32)
    for r in range(points):
        low = span * r // 128 * 128
        high = min(-(-(span * r + span) // 128) * 128, points * span)
        at = span * r - low
        left = (l0, l1, l2, l3)[r // 2]
        term = jnp.dot(left[r % 2], right[:, low:high], preferred_element_type=F32)
        total = total + term[:, at : at + span]
    out_ref[...] = total


def product(left, planes):
    _, side, lanes = left[0].shape
    span = planes[0].shape[1]
    return pl.pallas_call(
        product_kernel,
        out_shape=jax.ShapeDtypeStruct((side, span // 8), F32),
        in_specs=[pl.BlockSpec(memory_space=pltpu.VMEM)] * 8,
        out_specs=pl.BlockSpec(memory_space=pltpu.VMEM),
        scratch_shapes=[pltpu.VMEM((lanes, span), BF)],
        compiler_params=pltpu.CompilerParams(vmem_limit_bytes=12 * 1024 * 1024),
        interpret=INTERPRET,
    )(*left, *planes)


def one_hot(spots, count):
    return (jnp.arange(count)[:, None] == spots[None, :]).astype(BF)


def shards(potential, basis, weights, coupling):
    point = lax.axis_index("pt")
    pan = lax.axis_index("pan")
    core = pan % 2
    chip = pan // 2
    x, y, z = point // 2, chip // 4, chip % 4
    second = jnp.where(core == 0, y, z)
    first = jnp.where(core == 0, z, y)
    rows = potential[0]
    panel = basis.T
    width, depth = panel.shape

    antisym = coupling - coupling.T
    offset = jnp.arange(8)
    order = (x + offset // 2) % 4 * 2 + (offset + point) % 2
    turned = jnp.take(antisym, order, axis=1)
    with jax.named_scope("basis_line"):
        line = jnp.concatenate(gather_line(panel, along(True, True)), 0)
    with jax.named_scope("rows_pair"):
        line, fetched, other_rows, turned = lax.optimization_barrier(
            (line, send(panel, FAR), send(rows, CORE), turned)
        )
        chip_rows = jnp.where(
            core == 0, jnp.concatenate([rows, other_rows], 0), jnp.concatenate([other_rows, rows], 0)
        )
        chip_rows = lax.optimization_barrier(chip_rows)
    with jax.named_scope("basis_plane"):
        plane = along(False, True)
        near = send(line, plane(DOWN)), send(line, plane(UP))
        shared = [fetched] + [send(fetched, CROSS(step)) for step in (DOWN, TWO, UP)]
    with jax.named_scope("projected"):
        project = lambda unit: nt(unit, chip_rows).astype(BF)
        near_parts = [project(unit) for unit in near]
        *shared, near_parts[0], near_parts[1] = lax.optimization_barrier((*shared, *near_parts))
        two = jnp.zeros((4, width, depth), BF)
        for offset_x, piece in enumerate(shared):
            two = lax.dynamic_update_index_in_dim(two, piece, (x + offset_x) % 4, 0)
        two = two.reshape(4 * width, depth)
        units = line, near[0], two, near[1]
        parts = project(line), near_parts[0], project(two), near_parts[1]
        parts = [unroll(part.reshape(4, width, -1), first) for part in parts]
        blocks = unroll(jnp.stack(parts), second)
        blocks = jnp.where(core == 0, blocks, blocks.transpose(1, 0, 2, 3)).reshape(16, width, -1)
    with jax.named_scope("projected_exchange"):
        got = lax.all_to_all(blocks, "pan", 0, 0, axis_index_groups=CHIPS, tiled=True)
        own = got.transpose(1, 0, 2).reshape(width, depth)
        both = jnp.concatenate([own, send(own, CORE)], 0)
    with jax.named_scope("channel"):
        channel = jnp.concatenate([nt(both, u).astype(BF) for u in units], 1)
    lanes = 16 * width
    with jax.named_scope("columns_exchange"):
        crossed = send(channel[width:], CORE)
        block = jnp.arange(2 * lanes) // width
        dy, dz = (block // 8 - y) % 4, (block // 2 % 4 - z) % 4
        spot = jnp.where(block % 2 == 0, dy * 4 + dz, dz * 4 + dy) * width + jnp.arange(2 * lanes) % width
        mine = block % 2 == core
        ordered = jnp.dot(channel[:width], one_hot(jnp.where(mine, spot, -1), lanes), preferred_element_type=F32)
        ordered += jnp.dot(crossed, one_hot(jnp.where(mine, -1, spot), lanes), preferred_element_type=F32)
        ordered = ordered.astype(BF).reshape(width, 8, 4 * width).transpose(1, 0, 2)
        chosen = lax.all_to_all(ordered, "pt", 0, 0, tiled=True)
        chosen, channel = lax.optimization_barrier((chosen, channel))
        chosen = chosen.astype(F32)
        mixed = jnp.einsum("qr,qin->irn", turned, chosen, precision=lax.Precision.HIGHEST)
        mixed = mixed.astype(BF).reshape(width, -1)
        linear = jnp.einsum("q,qin->in", weights, chosen, precision=lax.Precision.HIGHEST)
    with jax.named_scope("mixed_line"):
        pieces = list(gather_line(mixed, along(True, False)))
        channel, pieces[1] = lax.optimization_barrier((channel, pieces[1]))
        pair = jnp.stack([channel, send(channel, HALF)])
        line = jnp.concatenate(pieces, 0)
    with jax.named_scope("mixed_plane"):
        planes = gather_line(line, along(False, False))
    with jax.named_scope("points"):
        left = gather_line(pair, CROSS)
    with jax.named_scope("product"):
        total = product(left, planes)
    with jax.named_scope("output"):
        return linear + total[:width] + send(total[width:], CORE)


def solution(mesh):
    in_specs = (P("pt", "pan", None), P(None, "pan"), P(), P())
    return jax.shard_map(shards, mesh=mesh, in_specs=in_specs, out_specs=P("pan", "pt"), check_vma=False)
```
